256 devices in a mesh: blk: 8 (over x_hi, y), grp: 32 (over x_lo, z, core).
Axes of the slice: x: 4 (x_hi: 2, x_lo: 2; x = x_hi * 2 + x_lo), y: 4, z: 8, core: 2. Of those that a mesh axis runs over, the one named last changes fastest.
Arguments:
- embeddings: bfloat16 [1024, 1024], P('blk'), may hold values from -8 to 8
- centroids: bfloat16 [524288, 1024], P(('blk', 'grp')), may hold values from -2 to 2
Outputs:
- centroid_sums: float32 [524288, 1024], P(('blk', 'grp'))
- centroid_mass: float32 [524288], P(('blk', 'grp'))
The draws below stay inside these ranges and needn't reach their ends.
All inputs are finite; a program needn't handle non-finite values.
Results may differ from the reference program's by a relative error of at most 0.014.
Values may be sent and summed in bfloat16 or wider, within the bound.
No kernel may reach another device: no remote copies, remote signals or barrier semaphores. Data moves between devices by JAX's collectives and lax.ppermute only.
A program may use at most 128 MiB of HBM per device.

```python
import jax
import jax.numpy as jnp
from jax import lax

D = 1024
CENT_DEV = 2048
ROWS = 1024
CENTROIDS = 524288


def centroid_rows(key, indices):

    def single(position):
        row_key = jax.random.fold_in(key, position)
        sign_key, scale_key = jax.random.split(row_key)
        sign_values = jnp.where(jax.random.bernoulli(sign_key, 0.5, (D,)), 1.0, -1.0).astype(jnp.float32)
        magnitude = jnp.exp(jax.random.uniform(scale_key, (), jnp.float32, jnp.log(0.7), jnp.log(1.4)))
        return sign_values * magnitude * D ** (-0.5)
    return jax.vmap(single)(indices)


def draw_centroids(key, part):
    return centroid_rows(key, jnp.arange(CENTROIDS, dtype=jnp.int32)).astype(jnp.bfloat16)


def draw_embeddings(key, part):
    key = jax.random.fold_in(key, 11)
    value_key = jax.random.fold_in(key, 0)
    values = jnp.clip(jax.random.normal(value_key, (ROWS, D), jnp.float32), -6.0, 6.0)
    return values.astype(jnp.bfloat16)


def setup_inputs(seed: int = 0) -> dict:
    arg_keys = jax.random.split(jax.random.key(seed), 3)
    embeddings = draw_embeddings(jax.random.fold_in(arg_keys[2], 71), 0)
    centroids = draw_centroids(jax.random.fold_in(arg_keys[2], 71), 0)
    return dict(embeddings=embeddings, centroids=centroids)


sharpness = 3.0


def block_scores(embeddings, block):
    squared = jnp.sum(jnp.square(block.astype(jnp.float32)), axis=1)
    product = jnp.dot(embeddings, block.T, preferred_element_type=jnp.float32)
    return sharpness * (product - 0.5 * squared[None, :])


def reference(embeddings, centroids):
    blocks = centroids.reshape(-1, CENT_DEV, D)

    def block_stats(block):
        scores = block_scores(embeddings, block)
        highest = jnp.max(scores, axis=1)
        totals = jnp.sum(jnp.exp(scores - highest[:, None]), axis=1)
        return highest, totals

    highs, totals = lax.map(block_stats, blocks)
    overall = jnp.max(highs, axis=0)
    log_norm = overall + jnp.log(jnp.sum(totals * jnp.exp(highs - overall[None, :]), axis=0))

    def accumulate(block):
        scores = block_scores(embeddings, block)
        weights = jnp.exp(scores - log_norm[:, None])
        rounded = weights.astype(jnp.bfloat16)
        sums = jnp.dot(rounded.T, embeddings, preferred_element_type=jnp.float32)
        return sums, jnp.sum(weights, axis=0)

    sums, masses = lax.map(accumulate, blocks)
    return sums.reshape(-1, D), masses.reshape(-1)
```

```python
import functools

import jax
import jax.numpy as jnp
from jax import lax
from jax.experimental import pallas as pl
from jax.experimental.pallas import tpu as pltpu
from jax.sharding import PartitionSpec as P

sharpness = 3.0
LOG2E = 1.4426950408889634
AXES = ("blk", "grp")
ROW_TILE = 256
CENT_TILE = 512
OUT_COLS = 256
OUT_ROWS = 1024
VMEM_LIMIT = 48 * 1024 * 1024

DEVICES = 256
X_HI, X_LO = 128, 16


def groups_by(key):
    groups = {}
    for device in range(DEVICES):
        groups.setdefault(key(device), []).append(device)
    return list(groups.values())


row_groups = groups_by(lambda d: (d % X_LO, (d // X_HI) ^ (d // X_LO % 2)))
plane_groups = groups_by(lambda d: d % X_LO)
column_groups = groups_by(lambda d: d // X_LO)


def in_vmem(value):
    return pltpu.with_memory_space_constraint(value, pltpu.VMEM)


def vmem_out(shape, dtype):
    return pltpu.VMEM(shape, dtype)


def score_kernel(first, *refs):
    if first:
        cents, rows, bias, probs, stats, scores = refs
    else:
        cents, rows, bias, earlier, probs, message, scores = refs
    cent_count, width = cents.shape
    row_count = rows.shape[0]
    cent_tiles = cent_count // CENT_TILE
    if first:
        def bias_step(i, carry):
            at = pl.ds(pl.multiple_of(i * CENT_TILE, CENT_TILE), CENT_TILE)
            block = cents[at, :].astype(jnp.float32)
            squared = jnp.sum(block * block, axis=1, keepdims=True)
            bias[at, :] = jnp.broadcast_to(squared * (-0.5 * sharpness * LOG2E), (CENT_TILE, 128))
            return carry
        lax.fori_loop(0, cent_tiles, bias_step, 0)
    found = []
    for j in range(row_count // ROW_TILE):
        row_block = rows[j * ROW_TILE:(j + 1) * ROW_TILE, :]

        def score_step(i, highest):
            at = pl.ds(pl.multiple_of(i * CENT_TILE, CENT_TILE), CENT_TILE)
            product = lax.dot_general(
                cents[at, :], row_block, (((1,), (1,)), ((), ())), preferred_element_type=jnp.float32
            )
            shift = jnp.concatenate([bias[at, :]] * (ROW_TILE // 128), axis=1)
            block = product * (sharpness * LOG2E) + shift
            scores[at, :] = block
            return jnp.maximum(highest, jnp.max(block.reshape(-1, 8, ROW_TILE), axis=0))

        highest = lax.fori_loop(
            0, cent_tiles, score_step, jnp.full((8, ROW_TILE), -jnp.inf, jnp.float32)
        )
        highest = jnp.max(highest, axis=0, keepdims=True)

        def exp_step(i, total):
            at = pl.ds(pl.multiple_of(i * CENT_TILE, CENT_TILE), CENT_TILE)
            block = jnp.exp2(scores[at, :] - highest)
            probs[at, j * ROW_TILE:(j + 1) * ROW_TILE] = block.astype(jnp.bfloat16)
            return total + jnp.sum(block.reshape(-1, 8, ROW_TILE), axis=0)

        total = lax.fori_loop(0, cent_tiles, exp_step, jnp.zeros((8, ROW_TILE), jnp.float32))
        found.append((highest, jnp.sum(total, axis=0, keepdims=True)))
    highest = jnp.concatenate([h for h, _ in found], axis=1)
    total = jnp.concatenate([t for _, t in found], axis=1)
    if first:
        stats[...] = jnp.concatenate([highest, total], axis=0)
    else:
        before = earlier[...]
        packed = jnp.concatenate([before[0:1], highest, before[1:2], total], axis=0)
        message[...] = jnp.broadcast_to(packed[None], message.shape)


def combined(received):
    parts = [received[k] for k in range(received.shape[0])]
    highest = functools.reduce(jnp.maximum, [p[0:2] for p in parts])
    total = functools.reduce(jnp.add, [p[2:4] * jnp.exp2(p[0:2] - highest) for p in parts])
    return highest, total


def ordered(core, pair):
    return jnp.where(core == 1, jnp.concatenate([pair[1:2], pair[0:1]], axis=0), pair)


def merge_kernel(core_ref, received, message):
    highest, total = combined(received)
    core = core_ref[0]
    packed = jnp.concatenate([ordered(core, highest), ordered(core, total)], axis=0)
    message[...] = jnp.broadcast_to(packed[None], message.shape)


def sum_kernel(core_ref, received, own, probs_a, probs_b, rows_a, rows_b, sums, mass, factors, weights):
    step, column = pl.program_id(0), pl.program_id(1)
    half = rows_a.shape[0]

    @pl.when(jnp.logical_and(step == 0, column == 0))
    def _():
        highest, total = combined(received)
        core = core_ref[0]
        highest, total = ordered(core, highest), ordered(core, total)
        factors[...] = jnp.exp2(own[0, 0:2] - highest) / total

    @pl.when(column == 0)
    def _():
        chunk = 128

        def weigh(i, carry):
            source = pl.ds(pl.multiple_of(step * OUT_ROWS + i * chunk, chunk), chunk)
            target = pl.ds(pl.multiple_of(i * chunk, chunk), chunk)
            wa = probs_a[source, :].astype(jnp.float32) * factors[0:1, :]
            wb = probs_b[source, :].astype(jnp.float32) * factors[1:2, :]
            weights[target, :half] = wa.astype(jnp.bfloat16)
            weights[target, half:] = wb.astype(jnp.bfloat16)
            part = wa + wb
            part = sum(part[:, k * 128:(k + 1) * 128] for k in range(half // 128))
            mass[pl.ds(step * (OUT_ROWS // chunk) + i, 1), :] = jnp.sum(part.T, axis=0, keepdims=True)
            return carry

        lax.fori_loop(0, OUT_ROWS // chunk, weigh, 0)

    at = pl.ds(pl.multiple_of(column * OUT_COLS, OUT_COLS), OUT_COLS)
    sums[...] = jnp.dot(
        weights[:, :half], rows_a[:, at], preferred_element_type=jnp.float32
    ) + jnp.dot(weights[:, half:], rows_b[:, at], preferred_element_type=jnp.float32)


def vmem_spec():
    return pl.BlockSpec(memory_space=pltpu.VMEM)


def params():
    return pltpu.CompilerParams(vmem_limit_bytes=VMEM_LIMIT)


def scored(cents, rows, bias=None, earlier=None):
    first = bias is None
    cent_count, half = cents.shape[0], rows.shape[0]
    probs = vmem_out((cent_count, half), jnp.bfloat16)
    if first:
        inputs = (cents, rows)
        outs = (vmem_out((cent_count, 128), jnp.float32), probs, vmem_out((2, half), jnp.float32))
    else:
        inputs = (cents, rows, bias, earlier)
        outs = (probs, vmem_out((len(plane_groups[0]), 4, half), jnp.float32))
    return pl.pallas_call(
        functools.partial(score_kernel, first),
        out_shape=outs,
        in_specs=[vmem_spec()] * len(inputs),
        out_specs=[vmem_spec()] * len(outs),
        scratch_shapes=[pltpu.VMEM((cent_count, ROW_TILE), jnp.float32)],
        compiler_params=params(),
    )(*[in_vmem(v) for v in inputs])


def merged(core, received):
    return pl.pallas_call(
        merge_kernel,
        out_shape=vmem_out((len(column_groups[0]),) + received.shape[1:], jnp.float32),
        in_specs=[pl.BlockSpec(memory_space=pltpu.SMEM), vmem_spec()],
        out_specs=vmem_spec(),
        compiler_params=params(),
    )(core, in_vmem(received))


def summed(core, received, own, probs_a, probs_b, rows_a, rows_b):
    cent_count, half = probs_a.shape
    width = rows_a.shape[1]
    inputs = (received, own, probs_a, probs_b, rows_a, rows_b)
    sums, mass = pl.pallas_call(
        sum_kernel,
        grid=(cent_count // OUT_ROWS, width // OUT_COLS),
        out_shape=(
            jax.ShapeDtypeStruct((cent_count, width), jnp.float32),
            jax.ShapeDtypeStruct((cent_count // 128, 128), jnp.float32),
        ),
        in_specs=[pl.BlockSpec(memory_space=pltpu.SMEM)] + [vmem_spec()] * len(inputs),
        out_specs=(
            pl.BlockSpec((OUT_ROWS, OUT_COLS), lambda i, j: (i, j)),
            vmem_spec(),
        ),
        scratch_shapes=[
            pltpu.VMEM((2, half), jnp.float32),
            pltpu.VMEM((OUT_ROWS, 2 * half), jnp.bfloat16),
        ],
        compiler_params=params(),
    )(core, *[in_vmem(v) for v in inputs])
    return sums, mass.reshape(-1)


def to_group(message, groups):
    return lax.all_to_all(message, AXES, 0, 0, tiled=True, axis_index_groups=groups)


def per_device(embeddings, centroids):
    core = lax.axis_index("grp") % 2
    core_ref = core.astype(jnp.int32).reshape(1)
    share = embeddings.shape[0] // 2
    mine = lax.dynamic_slice_in_dim(embeddings, core * share, share, 0)
    blocks = len(row_groups[0])
    rows_a = to_group(jnp.broadcast_to(mine[None], (blocks,) + mine.shape), row_groups)
    rows_a = rows_a.reshape(blocks * share, -1)
    rows_b = lax.ppermute(rows_a, AXES, [(d, d ^ 1) for d in range(DEVICES)])
    bias, probs_a, stats = scored(centroids, rows_a)
    probs_b, message = scored(centroids, rows_b, bias, stats)
    onward = merged(core_ref, to_group(message, plane_groups))
    received = to_group(onward, column_groups)
    return summed(core_ref, received, message, probs_a, probs_b, rows_a, rows_b)


def solution(mesh):
    in_specs = (P("blk", None), P(AXES, None))
    out_specs = (P(AXES, None), P(AXES))
    return jax.shard_map(
        per_device, mesh=mesh, in_specs=in_specs, out_specs=out_specs, check_vma=False
    )
```

```python
import functools

import jax
import jax.numpy as jnp
from jax import lax
from jax.experimental import pallas as pl
from jax.experimental.pallas import tpu as pltpu
from jax.sharding import PartitionSpec as P

sharpness = 3.0
LOG2E = 1.4426950408889634
SCALE = sharpness * LOG2E
AXES = ("blk", "grp")
LANES = 128
ROW_TILE = 256
CENT_TILE = 256
OUT_COLS = 512
OUT_ROWS = 256
MIB = 1024 * 1024
ARRIVALS = ((0, 256), (256, 256), (512, 512), (1024, 512), (1536, 512))

DEVICES = 256
X_HI, X_LO = 128, 16


def groups_by(key):
    groups = {}
    for device in range(DEVICES):
        groups.setdefault(key(device), []).append(device)
    return list(groups.values())


row_groups = groups_by(lambda d: (d % X_LO, (d // X_HI) ^ (d // X_LO % 2)))
plane_groups = groups_by(lambda d: d % X_LO)
column_groups = groups_by(lambda d: d // X_LO)


def in_vmem(value):
    return pltpu.with_memory_space_constraint(value, pltpu.VMEM)


def vmem_spec():
    return pl.BlockSpec(memory_space=pltpu.VMEM)


def part(i, size):
    return slice(i * size, (i + 1) * size)


def products(cents, rows, i, chunk):
    return lax.dot_general(
        cents[part(i, CENT_TILE), :],
        rows[part(chunk, ROW_TILE), :],
        (((1,), (1,)), ((), ())),
        preferred_element_type=jnp.float32,
    )


def shifted(block, bias):
    return block * SCALE + jnp.concatenate([bias] * (ROW_TILE // LANES), axis=1)


def fold(combine, block):
    return combine(block.reshape(-1, 8, block.shape[-1]), axis=0)


def no_highest():
    return jnp.full((8, ROW_TILE), -jnp.inf, jnp.float32)


def no_total():
    return jnp.zeros((8, ROW_TILE), jnp.float32)


def top(highest):
    return jnp.max(highest, axis=0, keepdims=True)


def whole(total):
    return jnp.sum(total, axis=0, keepdims=True)


def stacked(parts):
    return jnp.concatenate(
        [p[:, part(k, LANES)] for p in parts for k in range(p.shape[1] // LANES)], axis=0
    )


def exponentials(scores, highest, probs, i, column):
    block = jnp.exp2(scores[part(i, CENT_TILE), :] - highest)
    probs[part(i, CENT_TILE), part(column, ROW_TILE)] = block.astype(jnp.bfloat16)
    return fold(jnp.sum, block)


def first_kernel(source, rows, cents, bias, highs, scores_a, scores_b, arrived):
    copies = []
    for k, (start, size) in enumerate(ARRIVALS):
        at = pl.ds(start, size)
        copy = pltpu.make_async_copy(source.at[at, :], cents.at[at, :], arrived.at[k])
        copy.start()
        copies.append(copy)
    highest = [no_highest(), no_highest()]
    for copy, (start, size) in zip(copies, ARRIVALS):
        copy.wait()
        for i in range(start // CENT_TILE, (start + size) // CENT_TILE):
            block = cents[part(i, CENT_TILE), :].astype(jnp.float32)
            squared = jnp.sum(block * block, axis=1, keepdims=True)
            shift = jnp.broadcast_to(squared * (-0.5 * SCALE), (CENT_TILE, LANES))
            bias[part(i, CENT_TILE), :] = shift
            for chunk, scores in enumerate((scores_a, scores_b)):
                block = shifted(products(cents, rows, i, chunk), shift)
                scores[part(i, CENT_TILE), :] = block
                highest[chunk] = jnp.maximum(highest[chunk], fold(jnp.max, block))
    highs[...] = jnp.concatenate([top(h) for h in highest], axis=0)


def second_kernel(
    cents, rows, bias, highs, scores_a, scores_b, probs, own, message, scores_c, scores_d
):
    tiles = cents.shape[0] // CENT_TILE

    def step(chunk, scores, known):
        highest, totals = no_highest(), [no_total() for _ in known]
        for i in range(tiles):
            block = shifted(products(cents, rows, i, chunk), bias[part(i, CENT_TILE), :])
            scores[part(i, CENT_TILE), :] = block
            highest = jnp.maximum(highest, fold(jnp.max, block))
            for k, (before, high, column) in enumerate(known):
                totals[k] = totals[k] + exponentials(before, high, probs, i, column)
        return top(highest), [whole(t) for t in totals]

    highest_a, highest_b = highs[0:1, :], highs[1:2, :]
    highest_c, (total_a, total_b) = step(
        0, scores_c, [(scores_a, highest_a, 0), (scores_b, highest_b, 1)]
    )
    highest_d, (total_c,) = step(1, scores_d, [(scores_c, highest_c, 2)])
    total = no_total()
    for i in range(tiles):
        total = total + exponentials(scores_d, highest_d, probs, i, 3)
    highest = stacked([highest_a, highest_b, highest_c, highest_d])
    total = stacked([total_a, total_b, total_c, whole(total)])
    own[...] = highest
    message[...] = jnp.broadcast_to((highest + jnp.log(total) * LOG2E)[None], message.shape)


def combined(received):
    parts = [received[k] for k in range(received.shape[0])]
    highest = functools.reduce(jnp.maximum, parts)
    total = functools.reduce(jnp.add, [jnp.exp2(p - highest) for p in parts])
    return highest, total


def ordered(core, rows):
    half = rows.shape[0] // 2
    return jnp.where(core == 1, jnp.concatenate([rows[half:], rows[:half]], axis=0), rows)


def merge_kernel(core, received, message):
    highest, total = combined(received)
    merged = ordered(core[0], highest + jnp.log(total) * LOG2E)
    message[...] = jnp.broadcast_to(merged[None], message.shape)


def sum_kernel(
    core, received, own, probs, rows_a, rows_b,
    sums, mass, scaled, out, masses, sent, mass_sent,
):
    cent_count, width = out.shape
    half = rows_a.shape[0]
    highest, total = combined(received)
    factors = jnp.exp2(own[...] - ordered(core[0], highest)) / ordered(core[0], total)
    pieces = [(j, i) for j in range(width // OUT_COLS) for i in range(cent_count // OUT_ROWS)]
    tiles = cent_count // LANES
    copies = []
    for step, (j, i) in enumerate(pieces):
        columns = part(j, OUT_COLS)
        if i == 0:
            for k in range(2 * half // LANES):
                rows = (rows_a, rows_b)[k * LANES // half]
                factor = jnp.broadcast_to(factors[k:k + 1, :], (LANES, LANES)).T
                block = rows[part(k % (half // LANES), LANES), columns].astype(jnp.float32)
                block = block * jnp.concatenate([factor] * (OUT_COLS // LANES), axis=1)
                scaled[part(k, LANES), columns] = block.astype(jnp.bfloat16)
        at = part(i, OUT_ROWS)
        out[at, columns] = jnp.dot(
            probs[at, :], scaled[:, columns], preferred_element_type=jnp.float32
        )
        copy = pltpu.make_async_copy(out.at[at, columns], sums.at[at, columns], sent.at[step])
        copy.start()
        copies.append(copy)
        for k in range(tiles * step // (len(pieces) - 2), min(tiles, tiles * (step + 1) // (len(pieces) - 2))):
            at = part(k, LANES)
            lanes = 0.0
            for c in range(2 * half // LANES):
                block = probs[at, part(c, LANES)].astype(jnp.float32)
                lanes = lanes + block * factors[c:c + 1, :]
            masses[k:k + 1, :] = jnp.sum(lanes.T, axis=0, keepdims=True)
        if step == len(pieces) - 2:
            copy = pltpu.make_async_copy(masses, mass, mass_sent.at[0])
            copy.start()
            copies.append(copy)
    for copy in copies:
        copy.wait()


def call(kernel, inputs, in_specs, outs, out_specs, scratch, limit):
    return pl.pallas_call(
        kernel,
        out_shape=outs,
        in_specs=in_specs,
        out_specs=out_specs,
        scratch_shapes=scratch,
        compiler_params=pltpu.CompilerParams(vmem_limit_bytes=limit),
    )(*inputs)


def first_scores(centroids, rows):
    count, width = centroids.shape
    outs = (
        pltpu.VMEM((count, width), centroids.dtype),
        pltpu.VMEM((count, LANES), jnp.float32),
        pltpu.VMEM((2, ROW_TILE), jnp.float32),
        pltpu.VMEM((count, ROW_TILE), jnp.float32),
        pltpu.VMEM((count, ROW_TILE), jnp.float32),
    )
    scratch = [pltpu.SemaphoreType.DMA((len(ARRIVALS),))]
    in_specs = [pl.BlockSpec(memory_space=pltpu.HBM), vmem_spec()]
    inputs = (pltpu.with_memory_space_constraint(centroids, pltpu.HBM), in_vmem(rows))
    return call(first_kernel, inputs, in_specs, outs, [vmem_spec()] * len(outs), scratch, 12 * MIB)


def second_scores(cents, rows, bias, highs, scores_a, scores_b):
    count = cents.shape[0]
    row_tiles = 4 * ROW_TILE // LANES
    outs = (
        pltpu.VMEM((count, 4 * ROW_TILE), jnp.bfloat16),
        pltpu.VMEM((row_tiles, LANES), jnp.float32),
        pltpu.VMEM((len(plane_groups[0]), row_tiles, LANES), jnp.float32),
    )
    inputs = [in_vmem(v) for v in (cents, rows, bias, highs, scores_a, scores_b)]
    scratch = [pltpu.VMEM((count, ROW_TILE), jnp.float32)] * 2
    return call(
        second_kernel, inputs, [vmem_spec()] * len(inputs), outs, [vmem_spec()] * len(outs), scratch, 12 * MIB
    )


def merged(core, received):
    outs = pltpu.VMEM((len(column_groups[0]),) + received.shape[1:], jnp.float32)
    in_specs = [pl.BlockSpec(memory_space=pltpu.SMEM), vmem_spec()]
    return call(merge_kernel, (core, in_vmem(received)), in_specs, outs, vmem_spec(), [], 4 * MIB)


def summed(core, received, own, probs, rows_a, rows_b):
    count, width = probs.shape[0], rows_a.shape[1]
    inputs = [in_vmem(v) for v in (received, own, probs, rows_a, rows_b)]
    outs = (
        jax.ShapeDtypeStruct((count, width), jnp.float32),
        jax.ShapeDtypeStruct((count // LANES, LANES), jnp.float32),
    )
    scratch = [
        pltpu.VMEM((2 * rows_a.shape[0], width), jnp.bfloat16),
        pltpu.VMEM((count, width), jnp.float32),
        pltpu.VMEM((count // LANES, LANES), jnp.float32),
        pltpu.SemaphoreType.DMA(((count // OUT_ROWS) * (width // OUT_COLS),)),
        pltpu.SemaphoreType.DMA((1,)),
    ]
    in_specs = [pl.BlockSpec(memory_space=pltpu.SMEM)] + [vmem_spec()] * len(inputs)
    sums, mass = call(
        sum_kernel, [core] + inputs, in_specs, outs, [pl.BlockSpec(memory_space=pl.ANY)] * 2, scratch, 16 * MIB
    )
    return sums, mass.reshape(-1)


def to_group(message, groups):
    return lax.all_to_all(message, AXES, 0, 0, tiled=True, axis_index_groups=groups)


def per_device(embeddings, centroids):
    core = lax.axis_index("grp") % 2
    core_ref = core.astype(jnp.int32).reshape(1)
    share = embeddings.shape[0] // 2
    mine = lax.dynamic_slice_in_dim(embeddings, core * share, share, 0)
    blocks = len(row_groups[0])
    rows_a = to_group(jnp.broadcast_to(mine[None], (blocks,) + mine.shape), row_groups)
    rows_a = rows_a.reshape(blocks * share, -1)
    rows_b = lax.ppermute(rows_a, AXES, [(d, d ^ 1) for d in range(DEVICES)])
    cents, bias, highs, scores_a, scores_b = first_scores(centroids, rows_a)
    probs, own, message = second_scores(cents, rows_b, bias, highs, scores_a, scores_b)
    onward = merged(core_ref, to_group(message, plane_groups))
    received = to_group(onward, column_groups)
    return summed(core_ref, received, own, probs, rows_a, rows_b)


def solution(mesh):
    in_specs = (P("blk", None), P(AXES, None))
    out_specs = (P(AXES, None), P(AXES))
    return jax.shard_map(
        per_device, mesh=mesh, in_specs=in_specs, out_specs=out_specs, check_vma=False
    )
```

```python
import functools

import jax
import jax.numpy as jnp
from jax import lax
from jax.experimental import pallas as pl
from jax.experimental.pallas import tpu as pltpu
from jax.sharding import PartitionSpec as P

sharpness = 3.0
LOG2E = 1.4426950408889634
SCALE = sharpness * LOG2E
AXES = ("blk", "grp")
LANES = 128
ROW_TILE = 256
CENT_TILE = 256
OUT_COLS = 512
OUT_ROWS = 256
MIB = 1024 * 1024
ARRIVALS = ((0, 256), (256, 256), (512, 512), (1024, 512), (1536, 512))

DEVICES = 256
X_HI, Y, X_LO = 128, 32, 16


def groups_by(key):
    groups = {}
    for device in range(DEVICES):
        groups.setdefault(key(device), []).append(device)
    return list(groups.values())


def y_step(steps):
    return [(d, d // X_HI * X_HI + (d + steps * Y) % X_HI) for d in range(DEVICES)]


x_step = [(d, d ^ X_HI ^ X_LO) for d in range(DEVICES)]
core_step = [(d, d ^ 1) for d in range(DEVICES)]
Y_STEPS = (2, 1, 3)
plane_groups = groups_by(lambda d: d % X_LO)
column_groups = groups_by(lambda d: d // X_LO)


def in_vmem(value):
    return pltpu.with_memory_space_constraint(value, pltpu.VMEM)


def vmem_spec():
    return pl.BlockSpec(memory_space=pltpu.VMEM)


def part(i, size):
    return slice(i * size, (i + 1) * size)


def products(cents, rows, i):
    return lax.dot_general(
        cents[part(i, CENT_TILE), :],
        rows[...],
        (((1,), (1,)), ((), ())),
        preferred_element_type=jnp.float32,
    )


def shifted(block, bias):
    return block * SCALE + jnp.concatenate([bias] * (ROW_TILE // LANES), axis=1)


def fold(combine, block):
    return combine(block.reshape(-1, 8, block.shape[-1]), axis=0)


def no_highest():
    return jnp.full((8, ROW_TILE), -jnp.inf, jnp.float32)


def no_total():
    return jnp.zeros((8, ROW_TILE), jnp.float32)


def top(highest):
    return jnp.max(highest, axis=0, keepdims=True)


def whole(total):
    return jnp.sum(total, axis=0, keepdims=True)


def stacked(parts):
    return jnp.concatenate(
        [p[:, part(k, LANES)] for p in parts for k in range(p.shape[1] // LANES)], axis=0
    )


def exponentials(scores, highest, probs, i, column):
    block = jnp.exp2(scores[part(i, CENT_TILE), :] - highest)
    probs[part(i, CENT_TILE), part(column, ROW_TILE)] = block.astype(jnp.bfloat16)
    return fold(jnp.sum, block)


def arrange_kernel(device, *refs):
    blocks, rows = refs[:1 + len(Y_STEPS)], refs[-1]
    size = blocks[0].shape[0]
    y = device[0] // Y % 4
    for steps, block in zip((0,) + Y_STEPS, blocks):
        at = pl.multiple_of((y + 4 - steps) % 4 * size, size)
        rows[pl.ds(at, size), :] = block[...]


def first_kernel(source, rows, cents, bias, high, scores, arrived):
    copies = []
    for k, (start, size) in enumerate(ARRIVALS):
        at = pl.ds(start, size)
        copy = pltpu.make_async_copy(source.at[at, :], cents.at[at, :], arrived.at[k])
        copy.start()
        copies.append(copy)
    highest = no_highest()
    for copy, (start, size) in zip(copies, ARRIVALS):
        copy.wait()
        for i in range(start // CENT_TILE, (start + size) // CENT_TILE):
            block = cents[part(i, CENT_TILE), :].astype(jnp.float32)
            squared = jnp.sum(block * block, axis=1, keepdims=True)
            shift = jnp.broadcast_to(squared * (-0.5 * SCALE), (CENT_TILE, LANES))
            bias[part(i, CENT_TILE), :] = shift
            block = shifted(products(cents, rows, i), shift)
            scores[part(i, CENT_TILE), :] = block
            highest = jnp.maximum(highest, fold(jnp.max, block))
    high[...] = top(highest)


def score_step(cents, rows, bias, scores, before, highest_before, probs, column):
    highest, total = no_highest(), no_total()
    for i in range(cents.shape[0] // CENT_TILE):
        block = shifted(products(cents, rows, i), bias[part(i, CENT_TILE), :])
        scores[part(i, CENT_TILE), :] = block
        highest = jnp.maximum(highest, fold(jnp.max, block))
        total = total + exponentials(before, highest_before, probs, i, column)
    return top(highest), whole(total)


def middle_kernel(
    cents, bias, rows_b, rows_c, scores_a, high, probs, stats, scores_c, scores_b
):
    highest_a = high[...]
    highest_b, total_a = score_step(cents, rows_b, bias, scores_b, scores_a, highest_a, probs, 0)
    highest_c, total_b = score_step(cents, rows_c, bias, scores_c, scores_b, highest_b, probs, 1)
    stats[...] = jnp.concatenate([highest_a, highest_b, highest_c, total_a, total_b], axis=0)


def last_kernel(
    device, cents, bias, rows_d, scores_c, stats, probs, own, message, scores_d
):
    highest_c = stats[2:3, :]
    highest_d, total_c = score_step(cents, rows_d, bias, scores_d, scores_c, highest_c, probs, 0)
    total_d = no_total()
    for i in range(cents.shape[0] // CENT_TILE):
        total_d = total_d + exponentials(scores_d, highest_d, probs, i, 1)
    highest = stacked([stats[0:1, :], stats[1:2, :], highest_c, highest_d])
    total = stacked([stats[3:4, :], stats[4:5, :], total_c, whole(total_d)])
    own[...] = highest
    sent = by_x(device[0], highest + jnp.log(total) * LOG2E)
    message[...] = jnp.broadcast_to(sent[None], message.shape)


def combined(received):
    parts = [received[k] for k in range(received.shape[0])]
    highest = functools.reduce(jnp.maximum, parts)
    total = functools.reduce(jnp.add, [jnp.exp2(p - highest) for p in parts])
    return highest, total


def by_x(device, rows):
    quarter = rows.shape[0] // 4
    q = [rows[part(k, quarter)] for k in range(4)]
    return jnp.where(device // X_HI == 1, jnp.concatenate([q[1], q[0], q[3], q[2]], axis=0), rows)


def by_core(device, rows):
    half = rows.shape[0] // 2
    return jnp.where(device % 2 == 1, jnp.concatenate([rows[half:], rows[:half]], axis=0), rows)


def merge_kernel(device, received, message):
    highest, total = combined(received)
    merged = by_core(device[0], highest + jnp.log(total) * LOG2E)
    message[...] = jnp.broadcast_to(merged[None], message.shape)


def sum_kernel(
    device, received, own, probs_ab, probs_cd, rows_a, rows_b, rows_c, rows_d,
    sums, mass, scaled, out, masses, sent, mass_sent,
):
    cent_count, width = out.shape
    row_blocks = (rows_a, rows_b, rows_c, rows_d)
    block_tiles = ROW_TILE // LANES
    highest, total = (by_x(device[0], by_core(device[0], v)) for v in combined(received))
    factors = jnp.exp2(own[...] - highest) / total
    pieces = [(j, i) for j in range(width // OUT_COLS) for i in range(cent_count // OUT_ROWS)]
    tiles = cent_count // LANES
    copies = []
    for step, (j, i) in enumerate(pieces):
        columns = part(j, OUT_COLS)
        if i == 0:
            for k in range(4 * block_tiles):
                rows = row_blocks[k // block_tiles]
                factor = jnp.broadcast_to(factors[k:k + 1, :], (LANES, LANES)).T
                block = rows[part(k % block_tiles, LANES), columns].astype(jnp.float32)
                block = block * jnp.concatenate([factor] * (OUT_COLS // LANES), axis=1)
                scaled[part(k, LANES), columns] = block.astype(jnp.bfloat16)
        at = part(i, OUT_ROWS)
        weights = jnp.concatenate([probs_ab[at, :], probs_cd[at, :]], axis=1)
        out[at, columns] = jnp.dot(
            weights, scaled[:, columns], preferred_element_type=jnp.float32
        )
        copy = pltpu.make_async_copy(out.at[at, columns], sums.at[at, columns], sent.at[step])
        copy.start()
        copies.append(copy)
        for k in range(tiles * step // (len(pieces) - 2), min(tiles, tiles * (step + 1) // (len(pieces) - 2))):
            at = part(k, LANES)
            lanes = 0.0
            for probs, first in ((probs_ab, 0), (probs_cd, 2 * block_tiles)):
                for c in range(2 * block_tiles):
                    block = probs[at, part(c, LANES)].astype(jnp.float32)
                    lanes = lanes + block * factors[first + c:first + c + 1, :]
            masses[k:k + 1, :] = jnp.sum(lanes.T, axis=0, keepdims=True)
        if step == len(pieces) - 2:
            copy = pltpu.make_async_copy(masses, mass, mass_sent.at[0])
            copy.start()
            copies.append(copy)
    for copy in copies:
        copy.wait()


def call(kernel, inputs, in_specs, outs, out_specs, scratch, limit):
    return pl.pallas_call(
        kernel,
        out_shape=outs,
        in_specs=in_specs,
        out_specs=out_specs,
        scratch_shapes=scratch,
        compiler_params=pltpu.CompilerParams(vmem_limit_bytes=limit),
    )(*inputs)


def smem_spec():
    return pl.BlockSpec(memory_space=pltpu.SMEM)


def vmem_call(kernel, device, inputs, outs, scratch, limit):
    inputs = [in_vmem(v) for v in inputs]
    in_specs = [vmem_spec()] * len(inputs)
    if device is not None:
        inputs, in_specs = [device] + inputs, [smem_spec()] + in_specs
    return call(kernel, inputs, in_specs, outs, [vmem_spec()] * len(outs), scratch, limit)


def arranged(device, blocks, after=()):
    size, width = blocks[0].shape
    outs = (pltpu.VMEM((len(blocks) * size, width), blocks[0].dtype),)
    return vmem_call(arrange_kernel, device, blocks + list(after), outs, [], 4 * MIB)[0]


def first_scores(centroids, rows):
    count, width = centroids.shape
    outs = (
        pltpu.VMEM((count, width), centroids.dtype),
        pltpu.VMEM((count, LANES), jnp.float32),
        pltpu.VMEM((1, ROW_TILE), jnp.float32),
        pltpu.VMEM((count, ROW_TILE), jnp.float32),
    )
    scratch = [pltpu.SemaphoreType.DMA((len(ARRIVALS),))]
    in_specs = [pl.BlockSpec(memory_space=pltpu.HBM), vmem_spec()]
    inputs = (pltpu.with_memory_space_constraint(centroids, pltpu.HBM), in_vmem(rows))
    return call(first_kernel, inputs, in_specs, outs, [vmem_spec()] * len(outs), scratch, 8 * MIB)


def middle_scores(cents, bias, rows_b, rows_c, scores_a, high):
    count = cents.shape[0]
    outs = (
        pltpu.VMEM((count, 2 * ROW_TILE), jnp.bfloat16),
        pltpu.VMEM((5, ROW_TILE), jnp.float32),
        pltpu.VMEM((count, ROW_TILE), jnp.float32),
    )
    scratch = [pltpu.VMEM((count, ROW_TILE), jnp.float32)]
    inputs = (cents, bias, rows_b, rows_c, scores_a, high)
    return vmem_call(middle_kernel, None, inputs, outs, scratch, 8 * MIB)


def last_scores(device, cents, bias, rows_d, scores_c, stats):
    count = cents.shape[0]
    row_tiles = 4 * ROW_TILE // LANES
    outs = (
        pltpu.VMEM((count, 2 * ROW_TILE), jnp.bfloat16),
        pltpu.VMEM((row_tiles, LANES), jnp.float32),
        pltpu.VMEM((len(plane_groups[0]), row_tiles, LANES), jnp.float32),
    )
    scratch = [pltpu.VMEM((count, ROW_TILE), jnp.float32)]
    inputs = (cents, bias, rows_d, scores_c, stats)
    return vmem_call(last_kernel, device, inputs, outs, scratch, 8 * MIB)


def merged(device, received):
    outs = (pltpu.VMEM((len(column_groups[0]),) + received.shape[1:], jnp.float32),)
    return vmem_call(merge_kernel, device, (received,), outs, [], 4 * MIB)[0]


def summed(device, received, own, probs_ab, probs_cd, row_blocks):
    count, width = probs_ab.shape[0], row_blocks[0].shape[1]
    inputs = [in_vmem(v) for v in (received, own, probs_ab, probs_cd) + tuple(row_blocks)]
    outs = (
        jax.ShapeDtypeStruct((count, width), jnp.float32),
        jax.ShapeDtypeStruct((count // LANES, LANES), jnp.float32),
    )
    scratch = [
        pltpu.VMEM((4 * ROW_TILE, width), jnp.bfloat16),
        pltpu.VMEM((count, width), jnp.float32),
        pltpu.VMEM((count // LANES, LANES), jnp.float32),
        pltpu.SemaphoreType.DMA(((count // OUT_ROWS) * (width // OUT_COLS),)),
        pltpu.SemaphoreType.DMA((1,)),
    ]
    in_specs = [smem_spec()] + [vmem_spec()] * len(inputs)
    sums, mass = call(
        sum_kernel, [device] + inputs, in_specs, outs, [pl.BlockSpec(memory_space=pl.ANY)] * 2, scratch, 16 * MIB
    )
    return sums, mass.reshape(-1)


def to_group(message, groups):
    return lax.all_to_all(message, AXES, 0, 0, tiled=True, axis_index_groups=groups)


def per_device(embeddings, centroids):
    core = lax.axis_index("grp") % 2
    device = lax.axis_index(AXES).astype(jnp.int32).reshape(1)
    share = embeddings.shape[0] // 2
    mine = lax.dynamic_slice_in_dim(embeddings, core * share, share, 0)
    other = lax.ppermute(mine, AXES, x_step)
    near = [lax.ppermute(mine, AXES, y_step(steps)) for steps in Y_STEPS]
    far = [lax.ppermute(other, AXES, y_step(steps)) for steps in Y_STEPS]
    rows_a = arranged(device, [mine] + near)
    rows_c = lax.ppermute(rows_a, AXES, core_step)
    cents, bias, high, scores_a = first_scores(centroids, rows_a)
    rows_b = arranged(device, [other] + far, [high])
    rows_d = lax.ppermute(rows_b, AXES, core_step)
    probs_ab, stats, scores_c = middle_scores(cents, bias, rows_b, rows_c, scores_a, high)
    probs_cd, own, message = last_scores(device, cents, bias, rows_d, scores_c, stats)
    onward = merged(device, to_group(message, plane_groups))
    received = to_group(onward, column_groups)
    return summed(device, received, own, probs_ab, probs_cd, (rows_a, rows_b, rows_c, rows_d))


def solution(mesh):
    in_specs = (P("blk", None), P(AXES, None))
    out_specs = (P(AXES, None), P(AXES))
    return jax.shard_map(
        per_device, mesh=mesh, in_specs=in_specs, out_specs=out_specs, check_vma=False
    )
```

```python
import functools

import jax
import jax.numpy as jnp
from jax import lax
from jax.experimental import pallas as pl
from jax.experimental.pallas import tpu as pltpu
from jax.sharding import PartitionSpec as P

sharpness = 3.0
LOG2E = 1.4426950408889634
SCALE = sharpness * LOG2E
AXES = ("blk", "grp")
LANES = 128
ROW_TILE = 256
CENT_TILE = 256
OUT_COLS = 512
OUT_ROWS = 256
MIB = 1024 * 1024
ARRIVALS = ((0, 256), (256, 256), (512, 512), (1024, 512), (1536, 512))

DEVICES = 256
X_HI, Y, X_LO = 128, 32, 16


def groups_by(key):
    groups = {}
    for device in range(DEVICES):
        groups.setdefault(key(device), []).append(device)
    return list(groups.values())


def y_step(steps):
    return [(d, d // X_HI * X_HI + (d + steps * Y) % X_HI) for d in range(DEVICES)]


x_step = [(d, d ^ X_HI ^ X_LO) for d in range(DEVICES)]
core_step = [(d, d ^ 1) for d in range(DEVICES)]
Y_STEPS = (2, 1, 3)
plane_groups = groups_by(lambda d: d % X_LO)
column_groups = groups_by(lambda d: d // X_LO)


def in_vmem(value):
    return pltpu.with_memory_space_constraint(value, pltpu.VMEM)


def vmem_spec():
    return pl.BlockSpec(memory_space=pltpu.VMEM)


def part(i, size):
    return slice(i * size, (i + 1) * size)


def products(cents, rows, i):
    return lax.dot_general(
        cents[part(i, CENT_TILE), :],
        rows[...],
        (((1,), (1,)), ((), ())),
        preferred_element_type=jnp.float32,
    )


def shifted(block, bias):
    return block * SCALE + jnp.concatenate([bias] * (ROW_TILE // LANES), axis=1)


def fold(combine, block):
    return combine(block.reshape(-1, 8, block.shape[-1]), axis=0)


def no_highest():
    return jnp.full((8, ROW_TILE), -jnp.inf, jnp.float32)


def no_total():
    return jnp.zeros((8, ROW_TILE), jnp.float32)


def top(highest):
    return jnp.max(highest, axis=0, keepdims=True)


def whole(total):
    return jnp.sum(total, axis=0, keepdims=True)


def stacked(parts):
    return jnp.concatenate(
        [p[:, part(k, LANES)] for p in parts for k in range(p.shape[1] // LANES)], axis=0
    )


def exponentials(scores, highest, probs, i, column):
    block = jnp.exp2(scores[part(i, CENT_TILE), :] - highest)
    probs[part(i, CENT_TILE), part(column, ROW_TILE)] = block.astype(jnp.bfloat16)
    return fold(jnp.sum, block)


def arrange_kernel(device, *refs):
    blocks, rows = refs[:1 + len(Y_STEPS)], refs[-1]
    size = blocks[0].shape[0]
    y = device[0] // Y % 4
    for steps, block in zip((0,) + Y_STEPS, blocks):
        at = pl.multiple_of((y + 4 - steps) % 4 * size, size)
        rows[pl.ds(at, size), :] = block[...]


def bias_kernel(device, source, cents, bias, ready, arrived):
    ready[...] = jnp.zeros_like(ready)
    copies = []
    for k, (start, size) in enumerate(ARRIVALS):
        at = pl.ds(start, size)
        copy = pltpu.make_async_copy(source.at[at, :], cents.at[at, :], arrived.at[k])
        copy.start()
        copies.append(copy)
    for copy, (start, size) in zip(copies, ARRIVALS):
        copy.wait()
        for i in range(start // CENT_TILE, (start + size) // CENT_TILE):
            block = cents[part(i, CENT_TILE), :].astype(jnp.float32)
            squared = jnp.sum(block * block, axis=1, keepdims=True)
            bias[part(i, CENT_TILE), :] = jnp.broadcast_to(
                squared * (-0.5 * SCALE), (CENT_TILE, LANES)
            )


def first_kernel(cents, bias, rows, high, scores):
    highest = no_highest()
    for i in range(cents.shape[0] // CENT_TILE):
        block = shifted(products(cents, rows, i), bias[part(i, CENT_TILE), :])
        scores[part(i, CENT_TILE), :] = block
        highest = jnp.maximum(highest, fold(jnp.max, block))
    high[...] = top(highest)


def score_step(cents, rows, bias, scores, before, highest_before, probs, column):
    highest, total = no_highest(), no_total()
    for i in range(cents.shape[0] // CENT_TILE):
        block = shifted(products(cents, rows, i), bias[part(i, CENT_TILE), :])
        scores[part(i, CENT_TILE), :] = block
        highest = jnp.maximum(highest, fold(jnp.max, block))
        total = total + exponentials(before, highest_before, probs, i, column)
    return top(highest), whole(total)


def middle_kernel(
    cents, bias, rows_b, rows_c, scores_a, high, probs, stats, scores_c, scores_b
):
    highest_a = high[...]
    highest_b, total_a = score_step(cents, rows_b, bias, scores_b, scores_a, highest_a, probs, 0)
    highest_c, total_b = score_step(cents, rows_c, bias, scores_c, scores_b, highest_b, probs, 1)
    stats[...] = jnp.concatenate([highest_a, highest_b, highest_c, total_a, total_b], axis=0)


def last_kernel(
    device, cents, bias, rows_d, scores_c, stats, probs, own, message, scores_d
):
    highest_c = stats[2:3, :]
    highest_d, total_c = score_step(cents, rows_d, bias, scores_d, scores_c, highest_c, probs, 0)
    total_d = no_total()
    for i in range(cents.shape[0] // CENT_TILE):
        total_d = total_d + exponentials(scores_d, highest_d, probs, i, 1)
    highest = stacked([stats[0:1, :], stats[1:2, :], highest_c, highest_d])
    total = stacked([stats[3:4, :], stats[4:5, :], total_c, whole(total_d)])
    own[...] = highest
    sent = by_x(device[0], highest + jnp.log(total) * LOG2E)
    message[...] = jnp.broadcast_to(sent[None], message.shape)


def combined(received):
    parts = [received[k] for k in range(received.shape[0])]
    highest = functools.reduce(jnp.maximum, parts)
    total = functools.reduce(jnp.add, [jnp.exp2(p - highest) for p in parts])
    return highest, total


def by_x(device, rows):
    quarter = rows.shape[0] // 4
    q = [rows[part(k, quarter)] for k in range(4)]
    return jnp.where(device // X_HI == 1, jnp.concatenate([q[1], q[0], q[3], q[2]], axis=0), rows)


def by_core(device, rows):
    half = rows.shape[0] // 2
    return jnp.where(device % 2 == 1, jnp.concatenate([rows[half:], rows[:half]], axis=0), rows)


def merge_kernel(device, received, message):
    highest, total = combined(received)
    merged = by_core(device[0], highest + jnp.log(total) * LOG2E)
    message[...] = jnp.broadcast_to(merged[None], message.shape)


def sum_kernel(
    device, received, own, probs_ab, probs_cd, rows_a, rows_b, rows_c, rows_d,
    sums, mass, scaled, out, masses, sent, mass_sent,
):
    cent_count, width = out.shape
    row_blocks = (rows_a, rows_b, rows_c, rows_d)
    block_tiles = ROW_TILE // LANES
    highest, total = (by_x(device[0], by_core(device[0], v)) for v in combined(received))
    factors = jnp.exp2(own[...] - highest) / total
    pieces = [(j, i) for j in range(width // OUT_COLS) for i in range(cent_count // OUT_ROWS)]
    tiles = cent_count // LANES
    copies = []
    for step, (j, i) in enumerate(pieces):
        columns = part(j, OUT_COLS)
        if i == 0:
            for k in range(4 * block_tiles):
                rows = row_blocks[k // block_tiles]
                factor = jnp.broadcast_to(factors[k:k + 1, :], (LANES, LANES)).T
                block = rows[part(k % block_tiles, LANES), columns].astype(jnp.float32)
                block = block * jnp.concatenate([factor] * (OUT_COLS // LANES), axis=1)
                scaled[part(k, LANES), columns] = block.astype(jnp.bfloat16)
        at = part(i, OUT_ROWS)
        weights = jnp.concatenate([probs_ab[at, :], probs_cd[at, :]], axis=1)
        out[at, columns] = jnp.dot(
            weights, scaled[:, columns], preferred_element_type=jnp.float32
        )
        copy = pltpu.make_async_copy(out.at[at, columns], sums.at[at, columns], sent.at[step])
        copy.start()
        copies.append(copy)
        for k in range(tiles * step // (len(pieces) - 2), min(tiles, tiles * (step + 1) // (len(pieces) - 2))):
            at = part(k, LANES)
            lanes = 0.0
            for probs, first in ((probs_ab, 0), (probs_cd, 2 * block_tiles)):
                for c in range(2 * block_tiles):
                    block = probs[at, part(c, LANES)].astype(jnp.float32)
                    lanes = lanes + block * factors[first + c:first + c + 1, :]
            masses[k:k + 1, :] = jnp.sum(lanes.T, axis=0, keepdims=True)
        if step == len(pieces) - 2:
            copy = pltpu.make_async_copy(masses, mass, mass_sent.at[0])
            copy.start()
            copies.append(copy)
    for copy in copies:
        copy.wait()


def call(kernel, inputs, in_specs, outs, out_specs, scratch, limit):
    return pl.pallas_call(
        kernel,
        out_shape=outs,
        in_specs=in_specs,
        out_specs=out_specs,
        scratch_shapes=scratch,
        compiler_params=pltpu.CompilerParams(vmem_limit_bytes=limit),
    )(*inputs)


def smem_spec():
    return pl.BlockSpec(memory_space=pltpu.SMEM)


def vmem_call(kernel, device, inputs, outs, scratch, limit):
    inputs = [in_vmem(v) for v in inputs]
    in_specs = [vmem_spec()] * len(inputs)
    if device is not None:
        inputs, in_specs = [device] + inputs, [smem_spec()] + in_specs
    return call(kernel, inputs, in_specs, outs, [vmem_spec()] * len(outs), scratch, limit)


def arranged(device, blocks, after=()):
    size, width = blocks[0].shape
    outs = (pltpu.VMEM((len(blocks) * size, width), blocks[0].dtype),)
    return vmem_call(arrange_kernel, device, blocks + list(after), outs, [], 4 * MIB)[0]


def biased(device, centroids):
    count, width = centroids.shape
    outs = (
        pltpu.VMEM((count, width), centroids.dtype),
        pltpu.VMEM((count, LANES), jnp.float32),
        pltpu.VMEM((8, LANES), jnp.float32),
    )
    scratch = [pltpu.SemaphoreType.DMA((len(ARRIVALS),))]
    in_specs = [smem_spec(), pl.BlockSpec(memory_space=pltpu.HBM)]
    inputs = (device, pltpu.with_memory_space_constraint(centroids, pltpu.HBM))
    return call(bias_kernel, inputs, in_specs, outs, [vmem_spec()] * len(outs), scratch, 4 * MIB)


def first_scores(cents, bias, rows):
    count = cents.shape[0]
    outs = (pltpu.VMEM((1, ROW_TILE), jnp.float32), pltpu.VMEM((count, ROW_TILE), jnp.float32))
    return vmem_call(first_kernel, None, (cents, bias, rows), outs, [], 4 * MIB)


def middle_scores(cents, bias, rows_b, rows_c, scores_a, high):
    count = cents.shape[0]
    outs = (
        pltpu.VMEM((count, 2 * ROW_TILE), jnp.bfloat16),
        pltpu.VMEM((5, ROW_TILE), jnp.float32),
        pltpu.VMEM((count, ROW_TILE), jnp.float32),
    )
    scratch = [pltpu.VMEM((count, ROW_TILE), jnp.float32)]
    inputs = (cents, bias, rows_b, rows_c, scores_a, high)
    return vmem_call(middle_kernel, None, inputs, outs, scratch, 8 * MIB)


def last_scores(device, cents, bias, rows_d, scores_c, stats):
    count = cents.shape[0]
    row_tiles = 4 * ROW_TILE // LANES
    outs = (
        pltpu.VMEM((count, 2 * ROW_TILE), jnp.bfloat16),
        pltpu.VMEM((row_tiles, LANES), jnp.float32),
        pltpu.VMEM((len(plane_groups[0]), row_tiles, LANES), jnp.float32),
    )
    scratch = [pltpu.VMEM((count, ROW_TILE), jnp.float32)]
    inputs = (cents, bias, rows_d, scores_c, stats)
    return vmem_call(last_kernel, device, inputs, outs, scratch, 8 * MIB)


def merged(device, received):
    outs = (pltpu.VMEM((len(column_groups[0]),) + received.shape[1:], jnp.float32),)
    return vmem_call(merge_kernel, device, (received,), outs, [], 4 * MIB)[0]


def summed(device, received, own, probs_ab, probs_cd, row_blocks):
    count, width = probs_ab.shape[0], row_blocks[0].shape[1]
    inputs = [in_vmem(v) for v in (received, own, probs_ab, probs_cd) + tuple(row_blocks)]
    outs = (
        jax.ShapeDtypeStruct((count, width), jnp.float32),
        jax.ShapeDtypeStruct((count // LANES, LANES), jnp.float32),
    )
    scratch = [
        pltpu.VMEM((4 * ROW_TILE, width), jnp.bfloat16),
        pltpu.VMEM((count, width), jnp.float32),
        pltpu.VMEM((count // LANES, LANES), jnp.float32),
        pltpu.SemaphoreType.DMA(((count // OUT_ROWS) * (width // OUT_COLS),)),
        pltpu.SemaphoreType.DMA((1,)),
    ]
    in_specs = [smem_spec()] + [vmem_spec()] * len(inputs)
    sums, mass = call(
        sum_kernel, [device] + inputs, in_specs, outs, [pl.BlockSpec(memory_space=pl.ANY)] * 2, scratch, 16 * MIB
    )
    return sums, mass.reshape(-1)


def to_group(message, groups):
    return lax.all_to_all(message, AXES, 0, 0, tiled=True, axis_index_groups=groups)


def per_device(embeddings, centroids):
    core = lax.axis_index("grp") % 2
    device = lax.axis_index(AXES).astype(jnp.int32).reshape(1)
    share = embeddings.shape[0] // 2
    mine = lax.dynamic_slice_in_dim(embeddings, core * share, share, 0)
    other = lax.ppermute(mine, AXES, x_step)
    cents, bias, ready = biased(device, centroids)
    near = [lax.ppermute(mine, AXES, y_step(steps)) for steps in Y_STEPS]
    far = [lax.ppermute(other, AXES, y_step(steps)) for steps in Y_STEPS]
    rows_a = arranged(device, [mine] + near, [ready])
    rows_c = lax.ppermute(rows_a, AXES, core_step)
    high, scores_a = first_scores(cents, bias, rows_a)
    rows_b = arranged(device, [other] + far, [high, ready])
    rows_d = lax.ppermute(rows_b, AXES, core_step)
    probs_ab, stats, scores_c = middle_scores(cents, bias, rows_b, rows_c, scores_a, high)
    probs_cd, own, message = last_scores(device, cents, bias, rows_d, scores_c, stats)
    onward = merged(device, to_group(message, plane_groups))
    received = to_group(onward, column_groups)
    return summed(device, received, own, probs_ab, probs_cd, (rows_a, rows_b, rows_c, rows_d))


def solution(mesh):
    in_specs = (P("blk", None), P(AXES, None))
    out_specs = (P(AXES, None), P(AXES))
    return jax.shard_map(
        per_device, mesh=mesh, in_specs=in_specs, out_specs=out_specs, check_vma=False
    )
```

```python
import functools

import jax
import jax.numpy as jnp
from jax import lax
from jax.experimental import pallas as pl
from jax.experimental.pallas import tpu as pltpu
from jax.sharding import PartitionSpec as P

sharpness = 3.0
LOG2E = 1.4426950408889634
SCALE = sharpness * LOG2E
AXES = ("blk", "grp")
LANES = 128
ROW_TILE = 256
CENT_TILE = 256
OUT_COLS = 512
OUT_ROWS = 256
MIB = 1024 * 1024
ARRIVALS = ((0, 256), (256, 256), (512, 512), (1024, 512), (1536, 512))

DEVICES = 256
X_HI, Y, X_LO = 128, 32, 16


def groups_by(key):
    groups = {}
    for device in range(DEVICES):
        groups.setdefault(key(device), []).append(device)
    return list(groups.values())


def y_step(steps):
    return [(d, d // X_HI * X_HI + (d + steps * Y) % X_HI) for d in range(DEVICES)]


x_step = [(d, d ^ X_HI ^ X_LO) for d in range(DEVICES)]
core_step = [(d, d ^ 1) for d in range(DEVICES)]
Y_STEPS = (2, 3, 1)
plane_groups = groups_by(lambda d: d % X_LO)
column_groups = groups_by(lambda d: d // X_LO)


def in_vmem(value):
    return pltpu.with_memory_space_constraint(value, pltpu.VMEM)


def vmem_spec():
    return pl.BlockSpec(memory_space=pltpu.VMEM)


def part(i, size):
    return slice(i * size, (i + 1) * size)


def products(cents, rows, i):
    return lax.dot_general(
        cents[part(i, CENT_TILE), :],
        rows[...],
        (((1,), (1,)), ((), ())),
        preferred_element_type=jnp.float32,
    )


def shifted(block, bias):
    return block * SCALE + jnp.concatenate([bias] * (ROW_TILE // LANES), axis=1)


def fold(combine, block):
    return combine(block.reshape(-1, 8, block.shape[-1]), axis=0)


def no_highest():
    return jnp.full((8, ROW_TILE), -jnp.inf, jnp.float32)


def no_total():
    return jnp.zeros((8, ROW_TILE), jnp.float32)


def top(highest):
    return jnp.max(highest, axis=0, keepdims=True)


def whole(total):
    return jnp.sum(total, axis=0, keepdims=True)


def stacked(parts):
    return jnp.concatenate(
        [p[:, part(k, LANES)] for p in parts for k in range(p.shape[1] // LANES)], axis=0
    )


def exponentials(scores, highest, probs, i, column):
    block = jnp.exp2(scores[part(i, CENT_TILE), :] - highest)
    probs[part(i, CENT_TILE), part(column, ROW_TILE)] = block.astype(jnp.bfloat16)
    return fold(jnp.sum, block)


def arrange_kernel(device, *refs):
    blocks, rows = refs[:1 + len(Y_STEPS)], refs[-1]
    size = blocks[0].shape[0]
    y = device[0] // Y % 4
    for steps, block in zip((0,) + Y_STEPS, blocks):
        at = pl.multiple_of((y + 4 - steps) % 4 * size, size)
        rows[pl.ds(at, size), :] = block[...]


def bias_kernel(device, source, cents, bias, ready, arrived):
    ready[...] = jnp.zeros_like(ready)
    copies = []
    for k, (start, size) in enumerate(ARRIVALS):
        at = pl.ds(start, size)
        copy = pltpu.make_async_copy(source.at[at, :], cents.at[at, :], arrived.at[k])
        copy.start()
        copies.append(copy)
    for copy, (start, size) in zip(copies, ARRIVALS):
        copy.wait()
        for i in range(start // CENT_TILE, (start + size) // CENT_TILE):
            block = cents[part(i, CENT_TILE), :].astype(jnp.float32)
            squared = jnp.sum(block * block, axis=1, keepdims=True)
            bias[part(i, CENT_TILE), :] = jnp.broadcast_to(
                squared * (-0.5 * SCALE), (CENT_TILE, LANES)
            )


def first_kernel(cents, bias, rows, high, scores):
    highest = no_highest()
    for i in range(cents.shape[0] // CENT_TILE):
        block = shifted(products(cents, rows, i), bias[part(i, CENT_TILE), :])
        scores[part(i, CENT_TILE), :] = block
        highest = jnp.maximum(highest, fold(jnp.max, block))
    high[...] = top(highest)


def score_step(cents, rows, bias, scores, before, highest_before, probs, column):
    highest, total = no_highest(), no_total()
    for i in range(cents.shape[0] // CENT_TILE):
        block = shifted(products(cents, rows, i), bias[part(i, CENT_TILE), :])
        scores[part(i, CENT_TILE), :] = block
        highest = jnp.maximum(highest, fold(jnp.max, block))
        total = total + exponentials(before, highest_before, probs, i, column)
    return top(highest), whole(total)


def middle_kernel(
    cents, bias, rows_b, rows_c, scores_a, high, probs, stats, scores_c, scores_b
):
    highest_a = high[...]
    highest_b, total_a = score_step(cents, rows_b, bias, scores_b, scores_a, highest_a, probs, 0)
    highest_c, total_b = score_step(cents, rows_c, bias, scores_c, scores_b, highest_b, probs, 1)
    stats[...] = jnp.concatenate([highest_a, highest_b, highest_c, total_a, total_b], axis=0)


def last_kernel(
    device, cents, bias, rows_d, scores_c, stats, probs, own, message, scores_d
):
    highest_c = stats[2:3, :]
    highest_d, total_c = score_step(cents, rows_d, bias, scores_d, scores_c, highest_c, probs, 0)
    total_d = no_total()
    for i in range(cents.shape[0] // CENT_TILE):
        total_d = total_d + exponentials(scores_d, highest_d, probs, i, 1)
    highest = stacked([stats[0:1, :], stats[1:2, :], highest_c, highest_d])
    total = stacked([stats[3:4, :], stats[4:5, :], total_c, whole(total_d)])
    own[...] = highest
    sent = by_x(device[0], highest + jnp.log(total) * LOG2E)
    message[...] = jnp.broadcast_to(sent[None], message.shape)


def combined(received):
    parts = [received[k] for k in range(received.shape[0])]
    highest = functools.reduce(jnp.maximum, parts)
    total = functools.reduce(jnp.add, [jnp.exp2(p - highest) for p in parts])
    return highest, total


def by_x(device, rows):
    quarter = rows.shape[0] // 4
    q = [rows[part(k, quarter)] for k in range(4)]
    return jnp.where(device // X_HI == 1, jnp.concatenate([q[1], q[0], q[3], q[2]], axis=0), rows)


def by_core(device, rows):
    half = rows.shape[0] // 2
    return jnp.where(device % 2 == 1, jnp.concatenate([rows[half:], rows[:half]], axis=0), rows)


def merge_kernel(device, received, message):
    highest, total = combined(received)
    merged = by_core(device[0], highest + jnp.log(total) * LOG2E)
    message[...] = jnp.broadcast_to(merged[None], message.shape)


def sum_kernel(
    device, received, own, probs_ab, probs_cd, rows_a, rows_b, rows_c, rows_d,
    sums, mass, scaled, out, masses, sent, mass_sent,
):
    cent_count, width = out.shape
    row_blocks = (rows_a, rows_b, rows_c, rows_d)
    block_tiles = ROW_TILE // LANES
    highest, total = (by_x(device[0], by_core(device[0], v)) for v in combined(received))
    factors = jnp.exp2(own[...] - highest) / total
    pieces = [(j, i) for j in range(width // OUT_COLS) for i in range(cent_count // OUT_ROWS)]
    tiles = cent_count // LANES
    copies = []
    for step, (j, i) in enumerate(pieces):
        columns = part(j, OUT_COLS)
        if i == 0:
            for k in range(4 * block_tiles):
                rows = row_blocks[k // block_tiles]
                factor = jnp.broadcast_to(factors[k:k + 1, :], (LANES, LANES)).T
                block = rows[part(k % block_tiles, LANES), columns].astype(jnp.float32)
                block = block * jnp.concatenate([factor] * (OUT_COLS // LANES), axis=1)
                scaled[part(k, LANES), columns] = block.astype(jnp.bfloat16)
        at = part(i, OUT_ROWS)
        weights = jnp.concatenate([probs_ab[at, :], probs_cd[at, :]], axis=1)
        out[at, columns] = jnp.dot(
            weights, scaled[:, columns], preferred_element_type=jnp.float32
        )
        copy = pltpu.make_async_copy(out.at[at, columns], sums.at[at, columns], sent.at[step])
        copy.start()
        copies.append(copy)
        for k in range(tiles * step // (len(pieces) - 2), min(tiles, tiles * (step + 1) // (len(pieces) - 2))):
            at = part(k, LANES)
            lanes = 0.0
            for probs, first in ((probs_ab, 0), (probs_cd, 2 * block_tiles)):
                for c in range(2 * block_tiles):
                    block = probs[at, part(c, LANES)].astype(jnp.float32)
                    lanes = lanes + block * factors[first + c:first + c + 1, :]
            masses[k:k + 1, :] = jnp.sum(lanes.T, axis=0, keepdims=True)
        if step == len(pieces) - 2:
            copy = pltpu.make_async_copy(masses, mass, mass_sent.at[0])
            copy.start()
            copies.append(copy)
    for copy in copies:
        copy.wait()


def call(kernel, inputs, in_specs, outs, out_specs, scratch, limit):
    return pl.pallas_call(
        kernel,
        out_shape=outs,
        in_specs=in_specs,
        out_specs=out_specs,
        scratch_shapes=scratch,
        compiler_params=pltpu.CompilerParams(vmem_limit_bytes=limit),
    )(*inputs)


def smem_spec():
    return pl.BlockSpec(memory_space=pltpu.SMEM)


def vmem_call(kernel, device, inputs, outs, scratch, limit):
    inputs = [in_vmem(v) for v in inputs]
    in_specs = [vmem_spec()] * len(inputs)
    if device is not None:
        inputs, in_specs = [device] + inputs, [smem_spec()] + in_specs
    return call(kernel, inputs, in_specs, outs, [vmem_spec()] * len(outs), scratch, limit)


def arranged(device, blocks, after=()):
    size, width = blocks[0].shape
    outs = (pltpu.VMEM((len(blocks) * size, width), blocks[0].dtype),)
    return vmem_call(arrange_kernel, device, blocks + list(after), outs, [], 4 * MIB)[0]


def biased(device, centroids):
    count, width = centroids.shape
    outs = (
        pltpu.VMEM((count, width), centroids.dtype),
        pltpu.VMEM((count, LANES), jnp.float32),
        pltpu.VMEM((8, LANES), jnp.float32),
    )
    scratch = [pltpu.SemaphoreType.DMA((len(ARRIVALS),))]
    in_specs = [smem_spec(), pl.BlockSpec(memory_space=pltpu.HBM)]
    inputs = (device, pltpu.with_memory_space_constraint(centroids, pltpu.HBM))
    return call(bias_kernel, inputs, in_specs, outs, [vmem_spec()] * len(outs), scratch, 4 * MIB)


def first_scores(cents, bias, rows):
    count = cents.shape[0]
    outs = (pltpu.VMEM((1, ROW_TILE), jnp.float32), pltpu.VMEM((count, ROW_TILE), jnp.float32))
    return vmem_call(first_kernel, None, (cents, bias, rows), outs, [], 4 * MIB)


def middle_scores(cents, bias, rows_b, rows_c, scores_a, high):
    count = cents.shape[0]
    outs = (
        pltpu.VMEM((count, 2 * ROW_TILE), jnp.bfloat16),
        pltpu.VMEM((5, ROW_TILE), jnp.float32),
        pltpu.VMEM((count, ROW_TILE), jnp.float32),
    )
    scratch = [pltpu.VMEM((count, ROW_TILE), jnp.float32)]
    inputs = (cents, bias, rows_b, rows_c, scores_a, high)
    return vmem_call(middle_kernel, None, inputs, outs, scratch, 8 * MIB)


def last_scores(device, cents, bias, rows_d, scores_c, stats):
    count = cents.shape[0]
    row_tiles = 4 * ROW_TILE // LANES
    outs = (
        pltpu.VMEM((count, 2 * ROW_TILE), jnp.bfloat16),
        pltpu.VMEM((row_tiles, LANES), jnp.float32),
        pltpu.VMEM((len(plane_groups[0]), row_tiles, LANES), jnp.float32),
    )
    scratch = [pltpu.VMEM((count, ROW_TILE), jnp.float32)]
    inputs = (cents, bias, rows_d, scores_c, stats)
    return vmem_call(last_kernel, device, inputs, outs, scratch, 8 * MIB)


def merged(device, received):
    outs = (pltpu.VMEM((len(column_groups[0]),) + received.shape[1:], jnp.float32),)
    return vmem_call(merge_kernel, device, (received,), outs, [], 4 * MIB)[0]


def summed(device, received, own, probs_ab, probs_cd, row_blocks):
    count, width = probs_ab.shape[0], row_blocks[0].shape[1]
    inputs = [in_vmem(v) for v in (received, own, probs_ab, probs_cd) + tuple(row_blocks)]
    outs = (
        jax.ShapeDtypeStruct((count, width), jnp.float32),
        jax.ShapeDtypeStruct((count // LANES, LANES), jnp.float32),
    )
    scratch = [
        pltpu.VMEM((4 * ROW_TILE, width), jnp.bfloat16),
        pltpu.VMEM((count, width), jnp.float32),
        pltpu.VMEM((count // LANES, LANES), jnp.float32),
        pltpu.SemaphoreType.DMA(((count // OUT_ROWS) * (width // OUT_COLS),)),
        pltpu.SemaphoreType.DMA((1,)),
    ]
    in_specs = [smem_spec()] + [vmem_spec()] * len(inputs)
    sums, mass = call(
        sum_kernel, [device] + inputs, in_specs, outs, [pl.BlockSpec(memory_space=pl.ANY)] * 2, scratch, 16 * MIB
    )
    return sums, mass.reshape(-1)


def to_group(message, groups):
    return lax.all_to_all(message, AXES, 0, 0, tiled=True, axis_index_groups=groups)


def per_device(embeddings, centroids):
    core = lax.axis_index("grp") % 2
    device = lax.axis_index(AXES).astype(jnp.int32).reshape(1)
    share = embeddings.shape[0] // 2
    mine = lax.dynamic_slice_in_dim(embeddings, core * share, share, 0)
    other = lax.ppermute(mine, AXES, x_step)
    cents, bias, ready = biased(device, centroids)
    near = [lax.ppermute(mine, AXES, y_step(steps)) for steps in Y_STEPS]
    far = [lax.ppermute(other, AXES, y_step(steps)) for steps in Y_STEPS]
    rows_a = arranged(device, [mine] + near, [ready])
    rows_c = lax.ppermute(rows_a, AXES, core_step)
    high, scores_a = first_scores(cents, bias, rows_a)
    rows_b = arranged(device, [other] + far, [high, ready])
    rows_d = lax.ppermute(rows_b, AXES, core_step)
    probs_ab, stats, scores_c = middle_scores(cents, bias, rows_b, rows_c, scores_a, high)
    probs_cd, own, message = last_scores(device, cents, bias, rows_d, scores_c, stats)
    onward = merged(device, to_group(message, plane_groups))
    received = to_group(onward, column_groups)
    return summed(device, received, own, probs_ab, probs_cd, (rows_a, rows_b, rows_c, rows_d))


def solution(mesh):
    in_specs = (P("blk", None), P(AXES, None))
    out_specs = (P(AXES, None), P(AXES))
    return jax.shard_map(
        per_device, mesh=mesh, in_specs=in_specs, out_specs=out_specs, check_vma=False
    )
```

```python
import functools

import jax
import jax.numpy as jnp
from jax import lax
from jax.experimental import pallas as pl
from jax.experimental.pallas import tpu as pltpu
from jax.sharding import PartitionSpec as P

sharpness = 3.0
LOG2E = 1.4426950408889634
SCALE = sharpness * LOG2E
AXES = ("blk", "grp")
LANES = 128
ROW_TILE = 256
CENT_TILE = 512
OUT_COLS = 512
OUT_ROWS = 256
MIB = 1024 * 1024
ARRIVALS = ((0, 256), (256, 256), (512, 512), (1024, 512), (1536, 512))

DEVICES = 256
X_HI, Y, X_LO = 128, 32, 16


def groups_by(key):
    groups = {}
    for device in range(DEVICES):
        groups.setdefault(key(device), []).append(device)
    return list(groups.values())


def y_step(steps):
    return [(d, d // X_HI * X_HI + (d + steps * Y) % X_HI) for d in range(DEVICES)]


x_step = [(d, d ^ X_HI ^ X_LO) for d in range(DEVICES)]
core_step = [(d, d ^ 1) for d in range(DEVICES)]
Y_STEPS = (2, 3, 1)
plane_groups = groups_by(lambda d: d % X_LO)
column_groups = groups_by(lambda d: d // X_LO)


def in_vmem(value):
    return pltpu.with_memory_space_constraint(value, pltpu.VMEM)


def vmem_spec():
    return pl.BlockSpec(memory_space=pltpu.VMEM)


def part(i, size):
    return slice(i * size, (i + 1) * size)


def products(cents, rows, i):
    return lax.dot_general(
        cents[part(i, CENT_TILE), :],
        rows[...],
        (((1,), (1,)), ((), ())),
        preferred_element_type=jnp.float32,
    )


def shifted(block, bias):
    return block * SCALE + jnp.concatenate([bias] * (ROW_TILE // LANES), axis=1)


def fold(combine, block):
    return combine(block.reshape(-1, 8, block.shape[-1]), axis=0)


def no_highest():
    return jnp.full((8, ROW_TILE), -jnp.inf, jnp.float32)


def no_total():
    return jnp.zeros((8, ROW_TILE), jnp.float32)


def top(highest):
    return jnp.max(highest, axis=0, keepdims=True)


def whole(total):
    return jnp.sum(total, axis=0, keepdims=True)


def stacked(parts):
    return jnp.concatenate(
        [p[:, part(k, LANES)] for p in parts for k in range(p.shape[1] // LANES)], axis=0
    )


def exponentials(scores, highest, probs, i, column):
    block = jnp.exp2(scores[part(i, CENT_TILE), :] - highest)
    probs[part(i, CENT_TILE), part(column, ROW_TILE)] = block.astype(jnp.bfloat16)
    return fold(jnp.sum, block)


def arrange_kernel(device, *refs):
    blocks, rows = refs[:1 + len(Y_STEPS)], refs[-1]
    size = blocks[0].shape[0]
    y = device[0] // Y % 4
    for steps, block in zip((0,) + Y_STEPS, blocks):
        at = pl.multiple_of((y + 4 - steps) % 4 * size, size)
        rows[pl.ds(at, size), :] = block[...]


def bias_kernel(device, source, cents, bias, ready, arrived):
    ready[...] = jnp.zeros_like(ready)
    copies = []
    for k, (start, size) in enumerate(ARRIVALS):
        at = pl.ds(start, size)
        copy = pltpu.make_async_copy(source.at[at, :], cents.at[at, :], arrived.at[k])
        copy.start()
        copies.append(copy)
    for copy, (start, size) in zip(copies, ARRIVALS):
        copy.wait()
        for i in range(start // CENT_TILE, (start + size) // CENT_TILE):
            block = cents[part(i, CENT_TILE), :].astype(jnp.float32)
            squared = jnp.sum(block * block, axis=1, keepdims=True)
            bias[part(i, CENT_TILE), :] = jnp.broadcast_to(
                squared * (-0.5 * SCALE), (CENT_TILE, LANES)
            )


def first_kernel(cents, bias, rows, high, scores):
    highest = no_highest()
    for i in range(cents.shape[0] // CENT_TILE):
        block = shifted(products(cents, rows, i), bias[part(i, CENT_TILE), :])
        scores[part(i, CENT_TILE), :] = block
        highest = jnp.maximum(highest, fold(jnp.max, block))
    high[...] = top(highest)


def score_step(cents, rows, bias, scores, before, highest_before, probs, column):
    highest, total = no_highest(), no_total()
    for i in range(cents.shape[0] // CENT_TILE):
        block = shifted(products(cents, rows, i), bias[part(i, CENT_TILE), :])
        scores[part(i, CENT_TILE), :] = block
        highest = jnp.maximum(highest, fold(jnp.max, block))
        total = total + exponentials(before, highest_before, probs, i, column)
    return top(highest), whole(total)


def middle_kernel(
    cents, bias, rows_b, rows_c, scores_a, high, probs, stats, scores_c, scores_b
):
    highest_a = high[...]
    highest_b, total_a = score_step(cents, rows_b, bias, scores_b, scores_a, highest_a, probs, 0)
    highest_c, total_b = score_step(cents, rows_c, bias, scores_c, scores_b, highest_b, probs, 1)
    stats[...] = jnp.concatenate([highest_a, highest_b, highest_c, total_a, total_b], axis=0)


def last_kernel(
    device, cents, bias, rows_d, scores_c, stats, probs, own, message, scores_d
):
    highest_c = stats[2:3, :]
    highest_d, total_c = score_step(cents, rows_d, bias, scores_d, scores_c, highest_c, probs, 0)
    total_d = no_total()
    for i in range(cents.shape[0] // CENT_TILE):
        total_d = total_d + exponentials(scores_d, highest_d, probs, i, 1)
    highest = stacked([stats[0:1, :], stats[1:2, :], highest_c, highest_d])
    total = stacked([stats[3:4, :], stats[4:5, :], total_c, whole(total_d)])
    own[...] = highest
    sent = by_x(device[0], highest + jnp.log(total) * LOG2E)
    message[...] = jnp.broadcast_to(sent[None], message.shape)


def combined(received):
    parts = [received[k] for k in range(received.shape[0])]
    highest = functools.reduce(jnp.maximum, parts)
    total = functools.reduce(jnp.add, [jnp.exp2(p - highest) for p in parts])
    return highest, total


def by_x(device, rows):
    quarter = rows.shape[0] // 4
    q = [rows[part(k, quarter)] for k in range(4)]
    return jnp.where(device // X_HI == 1, jnp.concatenate([q[1], q[0], q[3], q[2]], axis=0), rows)


def by_core(device, rows):
    half = rows.shape[0] // 2
    return jnp.where(device % 2 == 1, jnp.concatenate([rows[half:], rows[:half]], axis=0), rows)


def merge_kernel(device, received, message):
    highest, total = combined(received)
    merged = by_core(device[0], highest + jnp.log(total) * LOG2E)
    message[...] = jnp.broadcast_to(merged[None], message.shape)


def sum_kernel(
    device, received, own, probs_ab, probs_cd, rows_a, rows_b, rows_c, rows_d,
    sums, mass, scaled, out, masses, sent, mass_sent,
):
    cent_count, width = out.shape
    row_blocks = (rows_a, rows_b, rows_c, rows_d)
    block_tiles = ROW_TILE // LANES
    highest, total = (by_x(device[0], by_core(device[0], v)) for v in combined(received))
    factors = jnp.exp2(own[...] - highest) / total
    pieces = [(j, i) for j in range(width // OUT_COLS) for i in range(cent_count // OUT_ROWS)]
    tiles = cent_count // LANES
    copies = []
    for step, (j, i) in enumerate(pieces):
        columns = part(j, OUT_COLS)
        if i == 0:
            for k in range(4 * block_tiles):
                rows = row_blocks[k // block_tiles]
                factor = jnp.broadcast_to(factors[k:k + 1, :], (LANES, LANES)).T
                block = rows[part(k % block_tiles, LANES), columns].astype(jnp.float32)
                block = block * jnp.concatenate([factor] * (OUT_COLS // LANES), axis=1)
                scaled[part(k, LANES), columns] = block.astype(jnp.bfloat16)
        at = part(i, OUT_ROWS)
        weights = jnp.concatenate([probs_ab[at, :], probs_cd[at, :]], axis=1)
        out[at, columns] = jnp.dot(
            weights, scaled[:, columns], preferred_element_type=jnp.float32
        )
        copy = pltpu.make_async_copy(out.at[at, columns], sums.at[at, columns], sent.at[step])
        copy.start()
        copies.append(copy)
        for k in range(tiles * step // (len(pieces) - 2), min(tiles, tiles * (step + 1) // (len(pieces) - 2))):
            at = part(k, LANES)
            lanes = 0.0
            for probs, first in ((probs_ab, 0), (probs_cd, 2 * block_tiles)):
                for c in range(2 * block_tiles):
                    block = probs[at, part(c, LANES)].astype(jnp.float32)
                    lanes = lanes + block * factors[first + c:first + c + 1, :]
            masses[k:k + 1, :] = jnp.sum(lanes.T, axis=0, keepdims=True)
        if step == len(pieces) - 2:
            copy = pltpu.make_async_copy(masses, mass, mass_sent.at[0])
            copy.start()
            copies.append(copy)
    for copy in copies:
        copy.wait()


def call(kernel, inputs, in_specs, outs, out_specs, scratch, limit):
    return pl.pallas_call(
        kernel,
        out_shape=outs,
        in_specs=in_specs,
        out_specs=out_specs,
        scratch_shapes=scratch,
        compiler_params=pltpu.CompilerParams(vmem_limit_bytes=limit),
    )(*inputs)


def smem_spec():
    return pl.BlockSpec(memory_space=pltpu.SMEM)


def vmem_call(kernel, device, inputs, outs, scratch, limit):
    inputs = [in_vmem(v) for v in inputs]
    in_specs = [vmem_spec()] * len(inputs)
    if device is not None:
        inputs, in_specs = [device] + inputs, [smem_spec()] + in_specs
    return call(kernel, inputs, in_specs, outs, [vmem_spec()] * len(outs), scratch, limit)


def arranged(device, blocks, after=()):
    size, width = blocks[0].shape
    outs = (pltpu.VMEM((len(blocks) * size, width), blocks[0].dtype),)
    return vmem_call(arrange_kernel, device, blocks + list(after), outs, [], 4 * MIB)[0]


def biased(device, centroids):
    count, width = centroids.shape
    outs = (
        pltpu.VMEM((count, width), centroids.dtype),
        pltpu.VMEM((count, LANES), jnp.float32),
        pltpu.VMEM((8, LANES), jnp.float32),
    )
    scratch = [pltpu.SemaphoreType.DMA((len(ARRIVALS),))]
    in_specs = [smem_spec(), pl.BlockSpec(memory_space=pltpu.HBM)]
    inputs = (device, pltpu.with_memory_space_constraint(centroids, pltpu.HBM))
    return call(bias_kernel, inputs, in_specs, outs, [vmem_spec()] * len(outs), scratch, 4 * MIB)


def first_scores(cents, bias, rows):
    count = cents.shape[0]
    outs = (pltpu.VMEM((1, ROW_TILE), jnp.float32), pltpu.VMEM((count, ROW_TILE), jnp.float32))
    return vmem_call(first_kernel, None, (cents, bias, rows), outs, [], 4 * MIB)


def middle_scores(cents, bias, rows_b, rows_c, scores_a, high):
    count = cents.shape[0]
    outs = (
        pltpu.VMEM((count, 2 * ROW_TILE), jnp.bfloat16),
        pltpu.VMEM((5, ROW_TILE), jnp.float32),
        pltpu.VMEM((count, ROW_TILE), jnp.float32),
    )
    scratch = [pltpu.VMEM((count, ROW_TILE), jnp.float32)]
    inputs = (cents, bias, rows_b, rows_c, scores_a, high)
    return vmem_call(middle_kernel, None, inputs, outs, scratch, 8 * MIB)


def last_scores(device, cents, bias, rows_d, scores_c, stats):
    count = cents.shape[0]
    row_tiles = 4 * ROW_TILE // LANES
    outs = (
        pltpu.VMEM((count, 2 * ROW_TILE), jnp.bfloat16),
        pltpu.VMEM((row_tiles, LANES), jnp.float32),
        pltpu.VMEM((len(plane_groups[0]), row_tiles, LANES), jnp.float32),
    )
    scratch = [pltpu.VMEM((count, ROW_TILE), jnp.float32)]
    inputs = (cents, bias, rows_d, scores_c, stats)
    return vmem_call(last_kernel, device, inputs, outs, scratch, 8 * MIB)


def merged(device, received):
    outs = (pltpu.VMEM((len(column_groups[0]),) + received.shape[1:], jnp.float32),)
    return vmem_call(merge_kernel, device, (received,), outs, [], 4 * MIB)[0]


def summed(device, received, own, probs_ab, probs_cd, row_blocks):
    count, width = probs_ab.shape[0], row_blocks[0].shape[1]
    inputs = [in_vmem(v) for v in (received, own, probs_ab, probs_cd) + tuple(row_blocks)]
    outs = (
        jax.ShapeDtypeStruct((count, width), jnp.float32),
        jax.ShapeDtypeStruct((count // LANES, LANES), jnp.float32),
    )
    scratch = [
        pltpu.VMEM((4 * ROW_TILE, width), jnp.bfloat16),
        pltpu.VMEM((count, width), jnp.float32),
        pltpu.VMEM((count // LANES, LANES), jnp.float32),
        pltpu.SemaphoreType.DMA(((count // OUT_ROWS) * (width // OUT_COLS),)),
        pltpu.SemaphoreType.DMA((1,)),
    ]
    in_specs = [smem_spec()] + [vmem_spec()] * len(inputs)
    sums, mass = call(
        sum_kernel, [device] + inputs, in_specs, outs, [pl.BlockSpec(memory_space=pl.ANY)] * 2, scratch, 16 * MIB
    )
    return sums, mass.reshape(-1)


def to_group(message, groups):
    return lax.all_to_all(message, AXES, 0, 0, tiled=True, axis_index_groups=groups)


def per_device(embeddings, centroids):
    core = lax.axis_index("grp") % 2
    device = lax.axis_index(AXES).astype(jnp.int32).reshape(1)
    share = embeddings.shape[0] // 2
    mine = lax.dynamic_slice_in_dim(embeddings, core * share, share, 0)
    other = lax.ppermute(mine, AXES, x_step)
    cents, bias, ready = biased(device, centroids)
    near = [lax.ppermute(mine, AXES, y_step(steps)) for steps in Y_STEPS]
    far = [lax.ppermute(other, AXES, y_step(steps)) for steps in Y_STEPS]
    rows_a = arranged(device, [mine] + near, [ready])
    rows_c = lax.ppermute(rows_a, AXES, core_step)
    high, scores_a = first_scores(cents, bias, rows_a)
    rows_b = arranged(device, [other] + far, [high, ready])
    rows_d = lax.ppermute(rows_b, AXES, core_step)
    probs_ab, stats, scores_c = middle_scores(cents, bias, rows_b, rows_c, scores_a, high)
    probs_cd, own, message = last_scores(device, cents, bias, rows_d, scores_c, stats)
    onward = merged(device, to_group(message, plane_groups))
    received = to_group(onward, column_groups)
    return summed(device, received, own, probs_ab, probs_cd, (rows_a, rows_b, rows_c, rows_d))


def solution(mesh):
    in_specs = (P("blk", None), P(AXES, None))
    out_specs = (P(AXES, None), P(AXES))
    return jax.shard_map(
        per_device, mesh=mesh, in_specs=in_specs, out_specs=out_specs, check_vma=False
    )
```
